32 devices in a mesh: ga: 4 (over z), sa: 8 (over y, x, core).
Axes of the slice: x: 2, y: 2, z: 4, core: 2. Of those that a mesh axis runs over, the one named last changes fastest.
Arguments:
- slab: float32 [8, 64, 64, 512], P(None, None, 'sa', 'ga'), may hold values from -6 to 6
- factor: float32 [64, 64], P('sa'), may hold values from -0.75 to 0.75
Outputs:
- lower: float32 [512, 512], P('ga')
- basis: float32 [8, 64, 64, 512], P('ga', 'sa')
The draws below stay inside these ranges and needn't reach their ends.
All inputs are finite; a program needn't handle non-finite values.
Results may differ from the reference program's by a relative error of at most 0.000073.
Values sent between devices are 32-bit elements; how exact they have to be, the bound alone decides.
A program may use at most 128 MiB of HBM per device.

```python
import jax
import jax.numpy as jnp
from jax import lax

S = 8
R1 = 64
R2 = 64
N2 = 64
N3 = 512


def raised(drawn, stream_key, source, target, blocks, factor):
    def block_of(position):
        return (jnp.arange(drawn.shape[position]) // (drawn.shape[position] // blocks)).reshape((-1,) + (1,) * (drawn.ndim - 1 - position))

    first = jax.random.permutation(stream_key, blocks)[block_of(target)]
    other_side = (block_of(target) + blocks // 2) % blocks
    return jnp.where((block_of(source) == first) | (block_of(source) == other_side), factor * drawn, drawn)


def shard_levels(own_key, shape, split, smallest, high):
    def one(axis_at, shards_of):
        draws = jax.random.uniform(jax.random.fold_in(jax.random.fold_in(own_key, 6), axis_at), (shards_of,), jnp.float32, smallest / len(split), high / len(split))
        return jnp.repeat(jnp.exp(draws), shape[axis_at] // shards_of).reshape((-1,) + (1,) * (len(shape) - axis_at - 1))

    gain = one(*split[0])
    for cut in split[1:]:
        gain = gain * one(*cut)
    return gain


def noise(key, shape, width, bound, cuts=(), kind=jnp.bfloat16):
    gain = shard_levels(key, shape, cuts, -0.22, 0.18) if cuts else 1.0
    values = jax.random.normal(key, shape, jnp.float32) * width * gain
    return jnp.minimum(jnp.maximum(values, -bound), bound).astype(kind)


def heavy_noise(stream_key, shape, deviation, reach, shards, heavy, kind=jnp.bfloat16):
    array = deviation * jax.random.normal(stream_key, shape, jnp.float32)
    if shards:
        array = array * shard_levels(stream_key, shape, shards, -0.22, 0.18)
    return jnp.clip(raised(array, jax.random.fold_in(stream_key, 3), *heavy), -reach, reach).astype(kind)


def setup_inputs(seed: int = 0) -> dict:
    key_of = jax.random.split(jax.random.key(seed), 3)
    slab = heavy_noise(key_of[0], (S, R1, N2, N3), 1.0, 6.0, ((2, 8), (3, 4)), (2, 1, 8, 2.0), jnp.float32)
    factor = noise(key_of[1], (N2, R2), N2 ** -0.5, 0.75, ((0, 8),), jnp.float32)
    return dict(slab=slab, factor=factor)


def reference(slab, factor):

    def one_species(block):
        return jnp.einsum('ajk,jr->ark', block, factor, precision=lax.Precision.HIGHEST)
    proj = lax.map(one_species, slab)
    count = S * R1 * R2
    unfold = proj.reshape(count, N3)
    gram = jnp.dot(unfold.T.astype(jnp.float32), unfold.astype(jnp.float32), precision=lax.Precision.HIGHEST, preferred_element_type=jnp.float32) / count
    lower = jnp.linalg.cholesky(gram)
    solved = jax.scipy.linalg.solve_triangular(lower, unfold.T, lower=True)
    basis = solved.T.reshape(S, R1, R2, N3)
    return (lower, basis)
```

```python
import functools

import jax
import jax.numpy as jnp
from jax import lax
from jax.experimental import pallas as pl
from jax.experimental.pallas import tpu as pltpu
from jax.sharding import PartitionSpec as P

MESH = pl.DeviceIdType.MESH
HIGHEST = lax.Precision.HIGHEST
LANES = 128
HALF = 64
STEP = 4


def tn(a, b):
    return lax.dot_general(a, b, (((0,), (0,)), ((), ())), precision=HIGHEST, preferred_element_type=jnp.float32)


def nn(a, b):
    return lax.dot_general(a, b, (((1,), (0,)), ((), ())), precision=HIGHEST, preferred_element_type=jnp.float32)


def split(x):
    hi = x.astype(jnp.bfloat16)
    return hi, (x - hi.astype(jnp.float32)).astype(jnp.bfloat16)


def mul16(a, b, dims):
    return lax.dot_general(a, b, (dims, ((), ())), preferred_element_type=jnp.float32)


def exchange_kernel(
    G, C, count,
    slab, factor, unfold, gram,
    fibres, whole_factor, acc, r1, s1, r2, s2, r3,
    a2a_send, a2a_recv, f_send, f_recv, own_sem,
    p1_send, p1_recv, p2_send, p2_recv, p3_send, p3_recv,
    g1_send, g1_recv, g2_send, g2_recv, g3_send, g3_recv,
):
    g, c = lax.axis_index("ga"), lax.axis_index("sa")
    D, chips = G * C, C // 2
    me = g * C + c
    core, chip = lax.rem(c, 2), c // 2
    s_here, a_here, depth, order = fibres.shape
    j_here, k_here = slab.shape[2], slab.shape[3]

    barrier = pltpu.get_barrier_semaphore()

    @pl.loop(1, D)
    def _(d):
        to = lax.rem(me + d, D)
        pl.semaphore_signal(barrier, inc=1, device_id=(to // C, lax.rem(to, C)), device_id_type=MESH)

    pl.semaphore_wait(barrier, D - 1)

    def remote(src, dst, send, recv, device):
        return pltpu.make_async_remote_copy(
            src_ref=src, dst_ref=dst, send_sem=send, recv_sem=recv, device_id=device, device_id_type=MESH
        )

    j_rows = pl.ds(pl.multiple_of(c * j_here, j_here), j_here)
    k_cols = pl.ds(pl.multiple_of(g * k_here, k_here), k_here)

    def factor_copy(d):
        return remote(factor, whole_factor.at[j_rows, :], f_send.at[d], f_recv.at[d], (g, lax.rem(c + d, C)))

    def chunk(to):
        return slab.at[pl.ds((to // C) * s_here, s_here), pl.ds(lax.rem(to, C) * a_here, a_here)]

    def slab_copy(d):
        to = lax.rem(me + d, D)
        return remote(
            chunk(to), fibres.at[:, :, j_rows, k_cols], a2a_send.at[d], a2a_recv.at[d], (to // C, lax.rem(to, C))
        )

    @pl.loop(1, C)
    def _(d):
        factor_copy(d).start()

    @pl.loop(1, D)
    def _(d):
        slab_copy(d).start()

    own = pltpu.make_async_copy(chunk(me), fibres.at[:, :, j_rows, k_cols], own_sem)
    own.start()
    whole_factor[j_rows, :] = factor[...]
    own.wait()

    @pl.loop(1, C)
    def _(d):
        factor_copy(d).wait()

    @pl.loop(1, D)
    def _(d):
        slab_copy(d).wait()

    @pl.loop(0, s_here * a_here)
    def _(i):
        s, a = i // a_here, lax.rem(i, a_here)
        unfold[s, a] = tn(whole_factor[...], fibres[s, a])

    columns = unfold[...].reshape(s_here * a_here * unfold.shape[2], order)
    hi, lo = split(columns)
    at = 0
    for left in range(0, order, LANES):
        low_hi, low_lo = hi[:, left:], lo[:, left:]
        this_hi, this_lo = hi[:, left:left + LANES], lo[:, left:left + LANES]
        contract = ((0,), (0,))
        part = mul16(low_hi, this_lo, contract) + mul16(low_lo, this_hi, contract)
        part = part + mul16(low_hi, this_hi, contract)
        acc[at:at + order - left, :] = part
        at += order - left
    if at < acc.shape[0]:
        acc[at:, :] = jnp.zeros((acc.shape[0] - at, LANES), jnp.float32)

    half, quarter = s1.shape[0], s2.shape[0]
    eighth = quarter // G

    def rows(start, size):
        return pl.ds(pl.multiple_of(start, 8), size)

    partner = (g, c + 1 - 2 * core)
    swap = remote(acc.at[rows((1 - core) * half, half)], r1, p1_send, p1_recv, partner)
    swap.start()
    swap.wait()
    s1[...] = acc[rows(core * half, half), :] + r1[...]

    def plane(d):
        to = lax.rem(chip + d, chips)
        return remote(s1.at[rows(to * quarter, quarter)], r2.at[d], p2_send.at[d], p2_recv.at[d], (g, to * 2 + core))

    for d in range(1, chips):
        plane(d).start()
    for d in range(1, chips):
        plane(d).wait()
    total = s1[rows(chip * quarter, quarter), :]
    for d in range(1, chips):
        total = total + r2[d]
    s2[...] = total

    def line(d):
        to = lax.rem(g + d, G)
        return remote(s2.at[rows(to * eighth, eighth)], r3.at[d], p3_send.at[d], p3_recv.at[d], (to, c))

    for d in range(1, G):
        line(d).start()
    for d in range(1, G):
        line(d).wait()
    total = s2[rows(g * eighth, eighth), :]
    for d in range(1, G):
        total = total + r3[d]
    mine = rows(core * half + chip * quarter + g * eighth, eighth)
    gram[mine, :] = total / count

    def line_back(d):
        return remote(gram.at[mine], gram.at[mine], g1_send.at[d], g1_recv.at[d], (lax.rem(g + d, G), c))

    for d in range(1, G):
        line_back(d).start()
    for d in range(1, G):
        line_back(d).wait()
    mine2 = rows(core * half + chip * quarter, quarter)

    def plane_back(d):
        to = lax.rem(chip + d, chips)
        return remote(gram.at[mine2], gram.at[mine2], g2_send.at[d], g2_recv.at[d], (g, to * 2 + core))

    for d in range(1, chips):
        plane_back(d).start()
    for d in range(1, chips):
        plane_back(d).wait()
    mine3 = rows(core * half, half)
    swap_back = remote(gram.at[mine3], gram.at[mine3], g3_send, g3_recv, partner)
    swap_back.start()
    swap_back.wait()


def eliminate(block):
    at_row = lax.broadcasted_iota(jnp.int32, (HALF, LANES), 0)
    at_lane = lax.broadcasted_iota(jnp.int32, (HALF, LANES), 1)
    m = jnp.concatenate([block, jnp.zeros((HALF, HALF), jnp.float32)], axis=1)
    m = jnp.where(at_lane == at_row + HALF, 1.0, m)
    for j in range(0, HALF, STEP):
        cols = [jnp.broadcast_to(m[:, j + t:j + t + 1], (HALF, LANES)) for t in range(STEP)]
        lines = [m[j + t:j + t + 1, :] for t in range(STEP)]
        small = [[cols[u][j + t:j + t + 1, :] for u in range(STEP)] for t in range(STEP)]
        for t in range(STEP):
            inverse = 1.0 / small[t][t]
            for u in range(t + 1, STEP):
                ratio = small[t][u] * inverse
                lines[u] = lines[u] - ratio * lines[t]
                cols[u] = cols[u] - ratio * cols[t]
                for v in range(u, STEP):
                    small[u][v] = small[u][v] - ratio * small[t][v]
            m = m - jnp.where(at_row > j + t, cols[t] * inverse, 0.0) * lines[t]
    pivot = jnp.sum(jnp.where(at_lane == at_row, m, 0.0), axis=1, keepdims=True)
    m = m * lax.rsqrt(pivot)
    upper = jnp.where(at_lane >= at_row, m, 0.0)
    return upper[:, :HALF], m[:, HALF:]


def factor_128(a):
    u1, w1 = eliminate(a[:HALF, :HALF])
    u12 = nn(w1, a[:HALF, HALF:])
    u2, w2 = eliminate(a[HALF:, HALF:] - tn(u12, u12))
    w21 = -nn(w2, tn(u12, w1))
    zero = jnp.zeros((HALF, HALF), jnp.float32)
    u = jnp.concatenate([jnp.concatenate([u1, u12], 1), jnp.concatenate([zero, u2], 1)], 0)
    w = jnp.concatenate([jnp.concatenate([w1, zero], 1), jnp.concatenate([w21, w2], 1)], 0)
    return u, w


def solve_kernel(unfold, gram, lower, basis, upper, inverse):
    order = upper.shape[0]
    upper[...] = jnp.zeros_like(upper)
    inverse[...] = jnp.zeros_like(inverse)
    at = 0
    for left in range(0, order, LANES):
        tall = gram[at:at + order - left, :]
        upper[left:left + LANES, left:] = tall.T
        at += order - left
    for i in range(0, order, LANES):
        n = i + LANES
        u, w = factor_128(upper[i:n, i:n])
        upper[i:n, i:n] = u
        if i:
            inverse[i:n, :i] = nn(w, inverse[i:n, :i])
        inverse[i:n, i:n] = w
        if n < order:
            right = nn(w, upper[i:n, n:])
            upper[i:n, n:] = right
            for t in range(n, order, LANES):
                block = right[:, t - n:t - n + LANES]
                upper[t:t + LANES, t:] -= tn(block, right[:, t - n:])
                inverse[t:t + LANES, :n] -= tn(block, inverse[i:n, :n])
    g = lax.axis_index("ga")
    mine = lower.shape[0]
    lower[...] = upper[:, pl.ds(pl.multiple_of(g * mine, mine), mine)].T
    w_hi, w_lo = split(inverse[...])
    contract = ((1,), (1,))

    @pl.loop(0, basis.shape[0] // LANES)
    def _(r):
        here = pl.ds(pl.multiple_of(r * LANES, LANES), LANES)
        hi, lo = split(unfold[here, :])
        out = mul16(hi, w_lo, contract) + mul16(lo, w_hi, contract)
        basis[here, :] = out + mul16(hi, w_hi, contract)


def shards(G, C, slab, factor):
    S, A, j_here, k_here = slab.shape
    R = factor.shape[1]
    depth, order = j_here * C, k_here * G
    s_here, a_here, chips = S // G, A // C, C // 2
    blocks = order // LANES
    cut = 8 * 2 * chips * G
    packed = -(-(blocks * (blocks + 1) // 2 * LANES) // cut) * cut
    half, quarter = packed // 2, packed // 2 // chips
    f32 = jnp.float32
    dma = pltpu.SemaphoreType.DMA
    unfold, gram = pl.pallas_call(
        functools.partial(exchange_kernel, G, C, S * A * R),
        out_shape=(
            jax.ShapeDtypeStruct((s_here, a_here, R, order), f32),
            jax.ShapeDtypeStruct((packed, LANES), f32),
        ),
        in_specs=[pl.BlockSpec(memory_space=pl.ANY), pl.BlockSpec(memory_space=pltpu.VMEM)],
        out_specs=(pl.BlockSpec(memory_space=pltpu.VMEM), pl.BlockSpec(memory_space=pltpu.VMEM)),
        scratch_shapes=[
            pltpu.VMEM((s_here, a_here, depth, order), f32),
            pltpu.VMEM((depth, R), f32),
            pltpu.VMEM((packed, LANES), f32),
            pltpu.VMEM((half, LANES), f32),
            pltpu.VMEM((half, LANES), f32),
            pltpu.VMEM((chips, quarter, LANES), f32),
            pltpu.VMEM((quarter, LANES), f32),
            pltpu.VMEM((G, quarter // G, LANES), f32),
            dma((G * C,)), dma((G * C,)), dma((C,)), dma((C,)), dma,
            dma, dma, dma((chips,)), dma((chips,)), dma((G,)), dma((G,)),
            dma((G,)), dma((G,)), dma((chips,)), dma((chips,)), dma, dma,
        ],
        compiler_params=pltpu.CompilerParams(
            collective_id=0, has_side_effects=True, vmem_limit_bytes=40 * 1024 * 1024
        ),
    )(slab, factor)
    rows = s_here * a_here * R
    lower, basis = pl.pallas_call(
        solve_kernel,
        out_shape=(
            jax.ShapeDtypeStruct((order // G, order), f32),
            jax.ShapeDtypeStruct((rows, order), f32),
        ),
        in_specs=[pl.BlockSpec(memory_space=pltpu.VMEM)] * 2,
        out_specs=(pl.BlockSpec(memory_space=pltpu.VMEM), pl.BlockSpec(memory_space=pltpu.VMEM)),
        scratch_shapes=[pltpu.VMEM((order, order), f32), pltpu.VMEM((order, order), f32)],
        compiler_params=pltpu.CompilerParams(vmem_limit_bytes=40 * 1024 * 1024),
    )(unfold.reshape(rows, order), gram)
    return lower, basis.reshape(s_here, a_here, R, order)


def solution(mesh):
    placed = (P(None, None, "sa", "ga"), P("sa", None))
    return jax.shard_map(
        functools.partial(shards, mesh.shape["ga"], mesh.shape["sa"]),
        mesh=mesh,
        in_specs=placed,
        out_specs=(P("ga", None), P("ga", "sa", None, None)),
        check_vma=False,
    )
```

```python
import functools

import jax
import jax.numpy as jnp
from jax import lax
from jax.experimental import pallas as pl
from jax.experimental.pallas import tpu as pltpu
from jax.sharding import PartitionSpec as P

MESH = pl.DeviceIdType.MESH
HIGHEST = lax.Precision.HIGHEST
LANES = 128
HALF = 64
STEP = 4
STRIDE = 11


def tn(a, b):
    return lax.dot_general(a, b, (((0,), (0,)), ((), ())), precision=HIGHEST, preferred_element_type=jnp.float32)


def nn(a, b):
    return lax.dot_general(a, b, (((1,), (0,)), ((), ())), precision=HIGHEST, preferred_element_type=jnp.float32)


def split(x):
    hi = x.astype(jnp.bfloat16)
    return hi, (x - hi.astype(jnp.float32)).astype(jnp.bfloat16)


def mul16(a, b, dims):
    return lax.dot_general(a, b, (dims, ((), ())), preferred_element_type=jnp.float32)


def exchange_kernel(
    G, C, parts, count,
    slab, factor, unfold, gram,
    fibres, whole_factor, acc, r1, s1, r2, s2, r3,
    a2a_send, a2a_recv, f_send, f_recv, own_sem,
    p1_send, p1_recv, p2_send, p2_recv, p3_send, p3_recv,
    g1_send, g1_recv, g2_send, g2_recv, g3_send, g3_recv,
):
    g, c = lax.axis_index("ga"), lax.axis_index("sa")
    D, chips = G * C, C // 2
    me = g * C + c
    core, chip = lax.rem(c, 2), c // 2
    s_here, a_here, depth, order = fibres.shape
    j_here, k_here = slab.shape[2], slab.shape[3]

    barrier = pltpu.get_barrier_semaphore()

    @pl.loop(1, D)
    def _(d):
        to = lax.rem(me + d, D)
        pl.semaphore_signal(barrier, inc=1, device_id=(to // C, lax.rem(to, C)), device_id_type=MESH)

    pl.semaphore_wait(barrier, D - 1)

    def remote(src, dst, send, recv, device):
        return pltpu.make_async_remote_copy(
            src_ref=src, dst_ref=dst, send_sem=send, recv_sem=recv, device_id=device, device_id_type=MESH
        )

    j_rows = pl.ds(pl.multiple_of(c * j_here, j_here), j_here)
    k_cols = pl.ds(pl.multiple_of(g * k_here, k_here), k_here)

    def factor_copy(d):
        return remote(factor, whole_factor.at[j_rows, :], f_send.at[d], f_recv.at[d], (g, lax.rem(c + d, C)))

    a_group = a_here // parts

    def chunk(s, a, to):
        return slab.at[(to // C) * s_here + s, pl.ds(lax.rem(to, C) * a_here + a, a_group)]

    def landing(s, a):
        return fibres.at[s, a:a + a_group, j_rows, k_cols]

    groups = [(s, a) for s in range(s_here) for a in range(0, a_here, a_group)]

    def slab_copy(q, d):
        to = lax.rem(me + lax.rem(d * STRIDE, D), D)
        return remote(
            chunk(*groups[q], to), landing(*groups[q]), a2a_send.at[q * D + d], a2a_recv.at[q * D + d],
            (to // C, lax.rem(to, C)),
        )

    @pl.loop(1, C)
    def _(d):
        factor_copy(d).start()

    for q in range(len(groups)):
        @pl.loop(1, D)
        def _(d):
            slab_copy(q, d).start()

    own = [pltpu.make_async_copy(chunk(*at, me), landing(*at), own_sem.at[q]) for q, at in enumerate(groups)]
    for copy in own:
        copy.start()
    whole_factor[j_rows, :] = factor[...]

    @pl.loop(1, C)
    def _(d):
        factor_copy(d).wait()

    packed = order * (order + LANES) // (2 * LANES)
    if packed < acc.shape[0]:
        acc[packed:, :] = jnp.zeros((acc.shape[0] - packed, LANES), jnp.float32)
    contract = ((0,), (0,))
    for q, (s, a) in enumerate(groups):
        own[q].wait()

        @pl.loop(1, D)
        def _(d):
            slab_copy(q, d).wait()

        pieces = [tn(whole_factor[...], fibres[s, a + i]) for i in range(a_group)]
        for i in range(a_group):
            unfold[s, a + i] = pieces[i]
        hi, lo = split(jnp.concatenate(pieces, axis=0))
        at = 0
        for left in range(0, order, LANES):
            this_hi, this_lo = hi[:, left:left + LANES], lo[:, left:left + LANES]
            part = mul16(hi[:, left:], this_lo, contract) + mul16(lo[:, left:], this_hi, contract)
            part = part + mul16(hi[:, left:], this_hi, contract)
            if q:
                part = part + acc[at:at + order - left, :]
            acc[at:at + order - left, :] = part
            at += order - left

    half, quarter = s1.shape[0], s2.shape[0]
    eighth = quarter // G

    def rows(start, size):
        return pl.ds(pl.multiple_of(start, 8), size)

    partner = (g, c + 1 - 2 * core)
    swap = remote(acc.at[rows((1 - core) * half, half)], r1, p1_send, p1_recv, partner)
    swap.start()
    swap.wait()
    s1[...] = acc[rows(core * half, half), :] + r1[...]

    def plane(d):
        to = lax.rem(chip + d, chips)
        return remote(s1.at[rows(to * quarter, quarter)], r2.at[d], p2_send.at[d], p2_recv.at[d], (g, to * 2 + core))

    for d in range(1, chips):
        plane(d).start()
    for d in range(1, chips):
        plane(d).wait()
    total = s1[rows(chip * quarter, quarter), :]
    for d in range(1, chips):
        total = total + r2[d]
    s2[...] = total

    def line(d):
        to = lax.rem(g + d, G)
        return remote(s2.at[rows(to * eighth, eighth)], r3.at[d], p3_send.at[d], p3_recv.at[d], (to, c))

    for d in range(1, G):
        line(d).start()
    for d in range(1, G):
        line(d).wait()
    total = s2[rows(g * eighth, eighth), :]
    for d in range(1, G):
        total = total + r3[d]
    mine = rows(core * half + chip * quarter + g * eighth, eighth)
    gram[mine, :] = total / count

    def line_back(d):
        return remote(gram.at[mine], gram.at[mine], g1_send.at[d], g1_recv.at[d], (lax.rem(g + d, G), c))

    for d in range(1, G):
        line_back(d).start()
    for d in range(1, G):
        line_back(d).wait()
    mine2 = rows(core * half + chip * quarter, quarter)

    def plane_back(d):
        to = lax.rem(chip + d, chips)
        return remote(gram.at[mine2], gram.at[mine2], g2_send.at[d], g2_recv.at[d], (g, to * 2 + core))

    for d in range(1, chips):
        plane_back(d).start()
    for d in range(1, chips):
        plane_back(d).wait()
    mine3 = rows(core * half, half)
    swap_back = remote(gram.at[mine3], gram.at[mine3], g3_send, g3_recv, partner)
    swap_back.start()
    swap_back.wait()


def eliminate(block):
    at_row = lax.broadcasted_iota(jnp.int32, (HALF, LANES), 0)
    at_lane = lax.broadcasted_iota(jnp.int32, (HALF, LANES), 1)
    m = jnp.concatenate([block, jnp.zeros((HALF, HALF), jnp.float32)], axis=1)
    m = jnp.where(at_lane == at_row + HALF, 1.0, m)
    for j in range(0, HALF, STEP):
        cols = [jnp.broadcast_to(m[:, j + t:j + t + 1], (HALF, LANES)) for t in range(STEP)]
        lines = [m[j + t:j + t + 1, :] for t in range(STEP)]
        small = [[cols[u][j + t:j + t + 1, :] for u in range(STEP)] for t in range(STEP)]
        for t in range(STEP):
            inverse = 1.0 / small[t][t]
            for u in range(t + 1, STEP):
                ratio = small[t][u] * inverse
                lines[u] = lines[u] - ratio * lines[t]
                cols[u] = cols[u] - ratio * cols[t]
                for v in range(u, STEP):
                    small[u][v] = small[u][v] - ratio * small[t][v]
            m = m - jnp.where(at_row > j + t, cols[t] * inverse, 0.0) * lines[t]
    pivot = jnp.sum(jnp.where(at_lane == at_row, m, 0.0), axis=1, keepdims=True)
    m = m * lax.rsqrt(pivot)
    upper = jnp.where(at_lane >= at_row, m, 0.0)
    return upper[:, :HALF], m[:, HALF:]


def factor_128(a):
    u1, w1 = eliminate(a[:HALF, :HALF])
    u12 = nn(w1, a[:HALF, HALF:])
    u2, w2 = eliminate(a[HALF:, HALF:] - tn(u12, u12))
    w21 = -nn(w2, tn(u12, w1))
    zero = jnp.zeros((HALF, HALF), jnp.float32)
    u = jnp.concatenate([jnp.concatenate([u1, u12], 1), jnp.concatenate([zero, u2], 1)], 0)
    w = jnp.concatenate([jnp.concatenate([w1, zero], 1), jnp.concatenate([w21, w2], 1)], 0)
    return u, w


def solve_kernel(unfold, gram, lower, basis, upper, inverse):
    order = upper.shape[0]
    upper[...] = jnp.zeros_like(upper)
    inverse[...] = jnp.zeros_like(inverse)
    at = 0
    for left in range(0, order, LANES):
        tall = gram[at:at + order - left, :]
        upper[left:left + LANES, left:] = tall.T
        at += order - left
    for i in range(0, order, LANES):
        n = i + LANES
        u, w = factor_128(upper[i:n, i:n])
        upper[i:n, i:n] = u
        if i:
            inverse[i:n, :i] = nn(w, inverse[i:n, :i])
        inverse[i:n, i:n] = w
        if n < order:
            right = nn(w, upper[i:n, n:])
            upper[i:n, n:] = right
            for t in range(n, order, LANES):
                block = right[:, t - n:t - n + LANES]
                upper[t:t + LANES, t:] -= tn(block, right[:, t - n:])
                inverse[t:t + LANES, :n] -= tn(block, inverse[i:n, :n])
    g = lax.axis_index("ga")
    mine = lower.shape[0]
    lower[...] = upper[:, pl.ds(pl.multiple_of(g * mine, mine), mine)].T
    w_hi, w_lo = split(inverse[...])
    contract = ((1,), (1,))

    @pl.loop(0, basis.shape[0] // LANES)
    def _(r):
        here = pl.ds(pl.multiple_of(r * LANES, LANES), LANES)
        hi, lo = split(unfold[here, :])
        out = mul16(hi, w_lo, contract) + mul16(lo, w_hi, contract)
        basis[here, :] = out + mul16(hi, w_hi, contract)


def shards(G, C, slab, factor):
    S, A, j_here, k_here = slab.shape
    R = factor.shape[1]
    depth, order = j_here * C, k_here * G
    s_here, a_here, chips = S // G, A // C, C // 2
    blocks = order // LANES
    cut = 8 * 2 * chips * G
    packed = -(-(blocks * (blocks + 1) // 2 * LANES) // cut) * cut
    half, quarter = packed // 2, packed // 2 // chips
    parts = 2 if a_here % 2 == 0 else 1
    sends = s_here * parts * G * C
    f32 = jnp.float32
    dma = pltpu.SemaphoreType.DMA
    unfold, gram = pl.pallas_call(
        functools.partial(exchange_kernel, G, C, parts, S * A * R),
        out_shape=(
            jax.ShapeDtypeStruct((s_here, a_here, R, order), f32),
            jax.ShapeDtypeStruct((packed, LANES), f32),
        ),
        in_specs=[pl.BlockSpec(memory_space=pl.ANY), pl.BlockSpec(memory_space=pltpu.VMEM)],
        out_specs=(pl.BlockSpec(memory_space=pltpu.VMEM), pl.BlockSpec(memory_space=pltpu.VMEM)),
        scratch_shapes=[
            pltpu.VMEM((s_here, a_here, depth, order), f32),
            pltpu.VMEM((depth, R), f32),
            pltpu.VMEM((packed, LANES), f32),
            pltpu.VMEM((half, LANES), f32),
            pltpu.VMEM((half, LANES), f32),
            pltpu.VMEM((chips, quarter, LANES), f32),
            pltpu.VMEM((quarter, LANES), f32),
            pltpu.VMEM((G, quarter // G, LANES), f32),
            dma((sends,)), dma((sends,)), dma((C,)), dma((C,)), dma((s_here * parts,)),
            dma, dma, dma((chips,)), dma((chips,)), dma((G,)), dma((G,)),
            dma((G,)), dma((G,)), dma((chips,)), dma((chips,)), dma, dma,
        ],
        compiler_params=pltpu.CompilerParams(
            collective_id=0, has_side_effects=True, vmem_limit_bytes=40 * 1024 * 1024
        ),
    )(slab, factor)
    rows = s_here * a_here * R
    lower, basis = pl.pallas_call(
        solve_kernel,
        out_shape=(
            jax.ShapeDtypeStruct((order // G, order), f32),
            jax.ShapeDtypeStruct((rows, order), f32),
        ),
        in_specs=[pl.BlockSpec(memory_space=pltpu.VMEM)] * 2,
        out_specs=(pl.BlockSpec(memory_space=pltpu.VMEM), pl.BlockSpec(memory_space=pltpu.VMEM)),
        scratch_shapes=[pltpu.VMEM((order, order), f32), pltpu.VMEM((order, order), f32)],
        compiler_params=pltpu.CompilerParams(vmem_limit_bytes=40 * 1024 * 1024),
    )(unfold.reshape(rows, order), gram)
    return lower, basis.reshape(s_here, a_here, R, order)


def solution(mesh):
    placed = (P(None, None, "sa", "ga"), P("sa", None))
    return jax.shard_map(
        functools.partial(shards, mesh.shape["ga"], mesh.shape["sa"]),
        mesh=mesh,
        in_specs=placed,
        out_specs=(P("ga", None), P("ga", "sa", None, None)),
        check_vma=False,
    )
```

```python
import functools

import jax
import jax.numpy as jnp
from jax import lax
from jax.experimental import pallas as pl
from jax.experimental.pallas import tpu as pltpu
from jax.sharding import PartitionSpec as P

MESH = pl.DeviceIdType.MESH
HIGHEST = lax.Precision.HIGHEST
LANES = 128
HALF = 64
STEP = 8
STRIDE = 11


def tn(a, b):
    return lax.dot_general(a, b, (((0,), (0,)), ((), ())), precision=HIGHEST, preferred_element_type=jnp.float32)


def nn(a, b):
    return lax.dot_general(a, b, (((1,), (0,)), ((), ())), precision=HIGHEST, preferred_element_type=jnp.float32)


def split(x):
    hi = x.astype(jnp.bfloat16)
    return hi, (x - hi.astype(jnp.float32)).astype(jnp.bfloat16)


def mul16(a, b, dims):
    return lax.dot_general(a, b, (dims, ((), ())), preferred_element_type=jnp.float32)


def exchange_kernel(
    G, C, parts, count,
    slab, factor, unfold, gram,
    fibres, whole_factor, acc, r1, s1, r2, s2, r3,
    a2a_send, a2a_recv, f_send, f_recv, own_sem,
    p1_send, p1_recv, p2_send, p2_recv, p3_send, p3_recv,
    g1_send, g1_recv, g2_send, g2_recv, g3_send, g3_recv,
):
    g, c = lax.axis_index("ga"), lax.axis_index("sa")
    D, chips = G * C, C // 2
    me = g * C + c
    core, chip = lax.rem(c, 2), c // 2
    s_here, a_here, depth, order = fibres.shape
    j_here, k_here = slab.shape[2], slab.shape[3]

    barrier = pltpu.get_barrier_semaphore()

    @pl.loop(1, D)
    def _(d):
        to = lax.rem(me + d, D)
        pl.semaphore_signal(barrier, inc=1, device_id=(to // C, lax.rem(to, C)), device_id_type=MESH)

    pl.semaphore_wait(barrier, D - 1)

    def remote(src, dst, send, recv, device):
        return pltpu.make_async_remote_copy(
            src_ref=src, dst_ref=dst, send_sem=send, recv_sem=recv, device_id=device, device_id_type=MESH
        )

    j_rows = pl.ds(pl.multiple_of(c * j_here, j_here), j_here)
    k_cols = pl.ds(pl.multiple_of(g * k_here, k_here), k_here)

    def factor_copy(d):
        return remote(factor, whole_factor.at[j_rows, :], f_send.at[d], f_recv.at[d], (g, lax.rem(c + d, C)))

    a_group = a_here // parts

    def chunk(s, a, to):
        return slab.at[(to // C) * s_here + s, pl.ds(lax.rem(to, C) * a_here + a, a_group)]

    def landing(s, a):
        return fibres.at[s, a:a + a_group, j_rows, k_cols]

    groups = [(s, a) for s in range(s_here) for a in range(0, a_here, a_group)]

    def slab_copy(q, d):
        to = lax.rem(me + lax.rem(d * STRIDE, D), D)
        return remote(
            chunk(*groups[q], to), landing(*groups[q]), a2a_send.at[q * D + d], a2a_recv.at[q * D + d],
            (to // C, lax.rem(to, C)),
        )

    @pl.loop(1, C)
    def _(d):
        factor_copy(d).start()

    for q in range(len(groups)):
        @pl.loop(1, D)
        def _(d):
            slab_copy(q, d).start()

    own = [pltpu.make_async_copy(chunk(*at, me), landing(*at), own_sem.at[q]) for q, at in enumerate(groups)]
    for copy in own:
        copy.start()
    whole_factor[j_rows, :] = factor[...]

    @pl.loop(1, C)
    def _(d):
        factor_copy(d).wait()

    packed = order * (order + LANES) // (2 * LANES)
    if packed < acc.shape[0]:
        acc[packed:, :] = jnp.zeros((acc.shape[0] - packed, LANES), jnp.float32)
    contract = ((0,), (0,))
    for q, (s, a) in enumerate(groups):
        own[q].wait()

        @pl.loop(1, D)
        def _(d):
            slab_copy(q, d).wait()

        pieces = [tn(whole_factor[...], fibres[s, a + i]) for i in range(a_group)]
        for i in range(a_group):
            unfold[s, a + i] = pieces[i]
        hi, lo = split(jnp.concatenate(pieces, axis=0))
        at = 0
        for left in range(0, order, LANES):
            this_hi, this_lo = hi[:, left:left + LANES], lo[:, left:left + LANES]
            part = mul16(hi[:, left:], this_lo, contract) + mul16(lo[:, left:], this_hi, contract)
            part = part + mul16(hi[:, left:], this_hi, contract)
            if q:
                part = part + acc[at:at + order - left, :]
            acc[at:at + order - left, :] = part
            at += order - left

    half, quarter = s1.shape[0], s2.shape[0]
    eighth = quarter // G

    def rows(start, size):
        return pl.ds(pl.multiple_of(start, 8), size)

    partner = (g, c + 1 - 2 * core)
    swap = remote(acc.at[rows((1 - core) * half, half)], r1, p1_send, p1_recv, partner)
    swap.start()
    swap.wait()
    s1[...] = acc[rows(core * half, half), :] + r1[...]

    def plane(d):
        to = lax.rem(chip + d, chips)
        return remote(s1.at[rows(to * quarter, quarter)], r2.at[d], p2_send.at[d], p2_recv.at[d], (g, to * 2 + core))

    for d in range(1, chips):
        plane(d).start()
    for d in range(1, chips):
        plane(d).wait()
    total = s1[rows(chip * quarter, quarter), :]
    for d in range(1, chips):
        total = total + r2[d]
    s2[...] = total

    def line(d):
        to = lax.rem(g + d, G)
        return remote(s2.at[rows(to * eighth, eighth)], r3.at[d], p3_send.at[d], p3_recv.at[d], (to, c))

    for d in range(1, G):
        line(d).start()
    for d in range(1, G):
        line(d).wait()
    total = s2[rows(g * eighth, eighth), :]
    for d in range(1, G):
        total = total + r3[d]
    mine = rows(core * half + chip * quarter + g * eighth, eighth)
    gram[mine, :] = total / count

    def line_back(d):
        return remote(gram.at[mine], gram.at[mine], g1_send.at[d], g1_recv.at[d], (lax.rem(g + d, G), c))

    for d in range(1, G):
        line_back(d).start()
    for d in range(1, G):
        line_back(d).wait()
    mine2 = rows(core * half + chip * quarter, quarter)

    def plane_back(d):
        to = lax.rem(chip + d, chips)
        return remote(gram.at[mine2], gram.at[mine2], g2_send.at[d], g2_recv.at[d], (g, to * 2 + core))

    for d in range(1, chips):
        plane_back(d).start()
    for d in range(1, chips):
        plane_back(d).wait()
    mine3 = rows(core * half, half)
    swap_back = remote(gram.at[mine3], gram.at[mine3], g3_send, g3_recv, partner)
    swap_back.start()
    swap_back.wait()


def eliminate(block):
    at_row = lax.broadcasted_iota(jnp.int32, (HALF, LANES), 0)
    at_lane = lax.broadcasted_iota(jnp.int32, (HALF, LANES), 1)
    m = jnp.concatenate([block, jnp.zeros((HALF, HALF), jnp.float32)], axis=1)
    m = jnp.where(at_lane == at_row + HALF, 1.0, m)
    for j in range(0, HALF, STEP):
        cols = [jnp.broadcast_to(m[:, j + t:j + t + 1], (HALF, LANES)) for t in range(STEP)]
        lines = [m[j + t:j + t + 1, :] for t in range(STEP)]
        small = [[cols[u][j + t:j + t + 1, :] for u in range(STEP)] for t in range(STEP)]
        for t in range(STEP):
            inverse = 1.0 / small[t][t]
            for u in range(t + 1, STEP):
                ratio = small[t][u] * inverse
                lines[u] = lines[u] - ratio * lines[t]
                cols[u] = cols[u] - ratio * cols[t]
                for v in range(u, STEP):
                    small[u][v] = small[u][v] - ratio * small[t][v]
            m = m - jnp.where(at_row > j + t, cols[t] * inverse, 0.0) * lines[t]
    pivot = jnp.sum(jnp.where(at_lane == at_row, m, 0.0), axis=1, keepdims=True)
    m = m * lax.rsqrt(pivot)
    upper = jnp.where(at_lane >= at_row, m, 0.0)
    return upper[:, :HALF], m[:, HALF:]


def factor_128(a):
    u1, w1 = eliminate(a[:HALF, :HALF])
    u12 = nn(w1, a[:HALF, HALF:])
    u2, w2 = eliminate(a[HALF:, HALF:] - tn(u12, u12))
    w21 = -nn(w2, tn(u12, w1))
    zero = jnp.zeros((HALF, HALF), jnp.float32)
    u = jnp.concatenate([jnp.concatenate([u1, u12], 1), jnp.concatenate([zero, u2], 1)], 0)
    w = jnp.concatenate([jnp.concatenate([w1, zero], 1), jnp.concatenate([w21, w2], 1)], 0)
    return u, w


def solve_kernel(unfold, gram, lower, basis, upper, inverse, x_hi, x_lo, out, out_sem):
    order = upper.shape[0]
    x_hi[...], x_lo[...] = split(unfold[...])
    copies = []
    upper[...] = jnp.zeros_like(upper)
    inverse[...] = jnp.zeros_like(inverse)
    at = 0
    for left in range(0, order, LANES):
        tall = gram[at:at + order - left, :]
        upper[left:left + LANES, left:] = tall.T
        at += order - left
    for i in range(0, order, LANES):
        n = i + LANES
        u, w = factor_128(upper[i:n, i:n])
        upper[i:n, i:n] = u
        if i:
            inverse[i:n, :i] = nn(w, inverse[i:n, :i])
        inverse[i:n, i:n] = w
        w_hi, w_lo = split(inverse[i:n, :n])
        contract = ((1,), (1,))
        part = mul16(x_hi[:, :n], w_lo, contract) + mul16(x_lo[:, :n], w_hi, contract)
        b = i // LANES
        out[b] = part + mul16(x_hi[:, :n], w_hi, contract)
        copies.append(pltpu.make_async_copy(out.at[b], basis.at[:, i:n], out_sem.at[b]))
        copies[-1].start()
        if n < order:
            right = nn(w, upper[i:n, n:])
            upper[i:n, n:] = right
            for t in range(n, order, LANES):
                block = right[:, t - n:t - n + LANES]
                upper[t:t + LANES, t:] -= tn(block, right[:, t - n:])
                inverse[t:t + LANES, :n] -= tn(block, inverse[i:n, :n])
    g = lax.axis_index("ga")
    mine = lower.shape[0]
    lower[...] = upper[:, pl.ds(pl.multiple_of(g * mine, mine), mine)].T
    for copy in copies:
        copy.wait()


def shards(G, C, slab, factor):
    S, A, j_here, k_here = slab.shape
    R = factor.shape[1]
    depth, order = j_here * C, k_here * G
    s_here, a_here, chips = S // G, A // C, C // 2
    blocks = order // LANES
    cut = 8 * 2 * chips * G
    packed = -(-(blocks * (blocks + 1) // 2 * LANES) // cut) * cut
    half, quarter = packed // 2, packed // 2 // chips
    parts = 2 if a_here % 2 == 0 else 1
    sends = s_here * parts * G * C
    f32 = jnp.float32
    dma = pltpu.SemaphoreType.DMA
    unfold, gram = pl.pallas_call(
        functools.partial(exchange_kernel, G, C, parts, S * A * R),
        out_shape=(
            jax.ShapeDtypeStruct((s_here, a_here, R, order), f32),
            jax.ShapeDtypeStruct((packed, LANES), f32),
        ),
        in_specs=[pl.BlockSpec(memory_space=pl.ANY), pl.BlockSpec(memory_space=pltpu.VMEM)],
        out_specs=(pl.BlockSpec(memory_space=pltpu.VMEM), pl.BlockSpec(memory_space=pltpu.VMEM)),
        scratch_shapes=[
            pltpu.VMEM((s_here, a_here, depth, order), f32),
            pltpu.VMEM((depth, R), f32),
            pltpu.VMEM((packed, LANES), f32),
            pltpu.VMEM((half, LANES), f32),
            pltpu.VMEM((half, LANES), f32),
            pltpu.VMEM((chips, quarter, LANES), f32),
            pltpu.VMEM((quarter, LANES), f32),
            pltpu.VMEM((G, quarter // G, LANES), f32),
            dma((sends,)), dma((sends,)), dma((C,)), dma((C,)), dma((s_here * parts,)),
            dma, dma, dma((chips,)), dma((chips,)), dma((G,)), dma((G,)),
            dma((G,)), dma((G,)), dma((chips,)), dma((chips,)), dma, dma,
        ],
        compiler_params=pltpu.CompilerParams(
            collective_id=0, has_side_effects=True, vmem_limit_bytes=40 * 1024 * 1024
        ),
    )(slab, factor)
    rows = s_here * a_here * R
    lower, basis = pl.pallas_call(
        solve_kernel,
        out_shape=(
            jax.ShapeDtypeStruct((order // G, order), f32),
            jax.ShapeDtypeStruct((rows, order), f32),
        ),
        in_specs=[pl.BlockSpec(memory_space=pltpu.VMEM)] * 2,
        out_specs=(pl.BlockSpec(memory_space=pltpu.VMEM), pl.BlockSpec(memory_space=pl.ANY)),
        scratch_shapes=[
            pltpu.VMEM((order, order), f32),
            pltpu.VMEM((order, order), f32),
            pltpu.VMEM((rows, order), jnp.bfloat16),
            pltpu.VMEM((rows, order), jnp.bfloat16),
            pltpu.VMEM((blocks, rows, LANES), f32),
            dma((blocks,)),
        ],
        compiler_params=pltpu.CompilerParams(vmem_limit_bytes=40 * 1024 * 1024),
    )(unfold.reshape(rows, order), gram)
    return lower, basis.reshape(s_here, a_here, R, order)


def solution(mesh):
    placed = (P(None, None, "sa", "ga"), P("sa", None))
    return jax.shard_map(
        functools.partial(shards, mesh.shape["ga"], mesh.shape["sa"]),
        mesh=mesh,
        in_specs=placed,
        out_specs=(P("ga", None), P("ga", "sa", None, None)),
        check_vma=False,
    )
```

```python
import functools

import jax
import jax.numpy as jnp
from jax import lax
from jax.experimental import pallas as pl
from jax.experimental.pallas import tpu as pltpu
from jax.sharding import PartitionSpec as P

MESH = pl.DeviceIdType.MESH
HIGHEST = lax.Precision.HIGHEST
LANES = 128
HALF = 64
STEP = 8
STRIDE = 11


def tn(a, b):
    return lax.dot_general(a, b, (((0,), (0,)), ((), ())), precision=HIGHEST, preferred_element_type=jnp.float32)


def nn(a, b):
    return lax.dot_general(a, b, (((1,), (0,)), ((), ())), precision=HIGHEST, preferred_element_type=jnp.float32)


def split(x):
    hi = x.astype(jnp.bfloat16)
    return hi, (x - hi.astype(jnp.float32)).astype(jnp.bfloat16)


def mul16(a, b, dims):
    return lax.dot_general(a, b, (dims, ((), ())), preferred_element_type=jnp.float32)


def exchange_kernel(
    G, C, parts, count,
    slab, factor, unfold, gram,
    fibres, whole_factor, acc, r1, s1, r2, s2, r3,
    a2a_send, a2a_recv, f_send, f_recv, own_sem,
    p1_send, p1_recv, p2_send, p2_recv, p3_send, p3_recv,
    g1_send, g1_recv, g2_send, g2_recv, g3_send, g3_recv,
):
    g, c = lax.axis_index("ga"), lax.axis_index("sa")
    D, chips = G * C, C // 2
    me = g * C + c
    core, chip = lax.rem(c, 2), c // 2
    s_here, a_here, depth, order = fibres.shape
    j_here, k_here = slab.shape[2], slab.shape[3]

    barrier = pltpu.get_barrier_semaphore()

    @pl.loop(1, D)
    def _(d):
        to = lax.rem(me + d, D)
        pl.semaphore_signal(barrier, inc=1, device_id=(to // C, lax.rem(to, C)), device_id_type=MESH)

    pl.semaphore_wait(barrier, D - 1)

    def remote(src, dst, send, recv, device):
        return pltpu.make_async_remote_copy(
            src_ref=src, dst_ref=dst, send_sem=send, recv_sem=recv, device_id=device, device_id_type=MESH
        )

    j_rows = pl.ds(pl.multiple_of(c * j_here, j_here), j_here)
    k_cols = pl.ds(pl.multiple_of(g * k_here, k_here), k_here)

    def factor_copy(d):
        return remote(factor, whole_factor.at[j_rows, :], f_send.at[d], f_recv.at[d], (g, lax.rem(c + d, C)))

    a_group = a_here // parts

    def chunk(s, a, to):
        return slab.at[(to // C) * s_here + s, pl.ds(lax.rem(to, C) * a_here + a, a_group)]

    def landing(s, a):
        return fibres.at[s, a:a + a_group, j_rows, k_cols]

    groups = [(s, a) for s in range(s_here) for a in range(0, a_here, a_group)]

    def slab_copy(q, d):
        to = lax.rem(me + lax.rem(d * STRIDE, D), D)
        return remote(
            chunk(*groups[q], to), landing(*groups[q]), a2a_send.at[q * D + d], a2a_recv.at[q * D + d],
            (to // C, lax.rem(to, C)),
        )

    @pl.loop(1, C)
    def _(d):
        factor_copy(d).start()

    for q in range(len(groups)):
        @pl.loop(1, D)
        def _(d):
            slab_copy(q, d).start()

    own = [pltpu.make_async_copy(chunk(*at, me), landing(*at), own_sem.at[q]) for q, at in enumerate(groups)]
    for copy in own:
        copy.start()
    whole_factor[j_rows, :] = factor[...]

    @pl.loop(1, C)
    def _(d):
        factor_copy(d).wait()

    packed = order * (order + LANES) // (2 * LANES)
    if packed < acc.shape[0]:
        acc[packed:, :] = jnp.zeros((acc.shape[0] - packed, LANES), jnp.float32)
    contract = ((0,), (0,))
    for q, (s, a) in enumerate(groups):
        own[q].wait()

        @pl.loop(1, D)
        def _(d):
            slab_copy(q, d).wait()

        pieces = [tn(whole_factor[...], fibres[s, a + i]) for i in range(a_group)]
        for i in range(a_group):
            unfold[s, a + i] = pieces[i]
        hi, lo = split(jnp.concatenate(pieces, axis=0))
        at = 0
        for left in range(0, order, LANES):
            this_hi, this_lo = hi[:, left:left + LANES], lo[:, left:left + LANES]
            part = mul16(hi[:, left:], this_lo, contract) + mul16(lo[:, left:], this_hi, contract)
            part = part + mul16(hi[:, left:], this_hi, contract)
            if q:
                part = part + acc[at:at + order - left, :]
            acc[at:at + order - left, :] = part
            at += order - left

    half, quarter = s1.shape[0], s2.shape[0]
    eighth = quarter // G

    def rows(start, size):
        return pl.ds(pl.multiple_of(start, 8), size)

    partner = (g, c + 1 - 2 * core)

    def swap(d):
        here = lax.rem(chip + d, chips) * quarter
        return remote(
            acc.at[rows((1 - core) * half + here, quarter)], r1.at[rows(here, quarter)],
            p1_send.at[d], p1_recv.at[d], partner,
        )

    def plane(d):
        to = lax.rem(chip + d, chips)
        return remote(s1.at[rows(to * quarter, quarter)], r2.at[d], p2_send.at[d], p2_recv.at[d], (g, to * 2 + core))

    for d in range(1, chips + 1):
        swap(d % chips).start()
    for d in range(1, chips + 1):
        swap(d % chips).wait_recv()
        here = lax.rem(chip + d, chips) * quarter
        s1[rows(here, quarter), :] = acc[rows(core * half + here, quarter), :] + r1[rows(here, quarter), :]
        if d < chips:
            plane(d).start()
    for d in range(1, chips):
        plane(d).wait()
    total = s1[rows(chip * quarter, quarter), :]
    for d in range(1, chips):
        total = total + r2[d]
    s2[...] = total

    def line(d):
        to = lax.rem(g + d, G)
        return remote(s2.at[rows(to * eighth, eighth)], r3.at[d], p3_send.at[d], p3_recv.at[d], (to, c))

    for d in range(1, G):
        line(d).start()
    for d in range(1, G):
        line(d).wait()
    total = s2[rows(g * eighth, eighth), :]
    for d in range(1, G):
        total = total + r3[d]
    mine = rows(core * half + chip * quarter + g * eighth, eighth)
    gram[mine, :] = total / count

    def line_back(d):
        return remote(gram.at[mine], gram.at[mine], g1_send.at[d], g1_recv.at[d], (lax.rem(g + d, G), c))

    def piece(z, d):
        owner = lax.rem(chip - d + chips, chips)
        return rows(core * half + owner * quarter + lax.rem(g - z + G, G) * eighth, eighth)

    def plane_back(z, d):
        to = lax.rem(chip + d, chips)
        sem = z * chips + d
        return remote(gram.at[piece(z, 0)], gram.at[piece(z, 0)], g2_send.at[sem], g2_recv.at[sem], (g, to * 2 + core))

    def swap_back(z, d):
        sem = z * chips + d
        return remote(gram.at[piece(z, d)], gram.at[piece(z, d)], g3_send.at[sem], g3_recv.at[sem], partner)

    for d in range(1, G):
        line_back(d).start()
    for z in range(G):
        if z:
            line_back(z).wait_recv()
        for d in range(1, chips):
            plane_back(z, d).start()
        swap_back(z, 0).start()
    for z in range(G):
        for d in range(1, chips):
            plane_back(z, d).wait_recv()
            swap_back(z, d).start()
    for d in range(1, G):
        line_back(d).wait_send()
    for d in range(chips):
        swap(d).wait_send()
    for z in range(G):
        for d in range(chips):
            if d:
                plane_back(z, d).wait_send()
            swap_back(z, d).wait()


def eliminate(block):
    at_row = lax.broadcasted_iota(jnp.int32, (HALF, LANES), 0)
    at_lane = lax.broadcasted_iota(jnp.int32, (HALF, LANES), 1)
    m = jnp.concatenate([block, jnp.zeros((HALF, HALF), jnp.float32)], axis=1)
    m = jnp.where(at_lane == at_row + HALF, 1.0, m)
    for j in range(0, HALF, STEP):
        cols = [jnp.broadcast_to(m[:, j + t:j + t + 1], (HALF, LANES)) for t in range(STEP)]
        lines = [m[j + t:j + t + 1, :] for t in range(STEP)]
        small = [[cols[u][j + t:j + t + 1, :] for u in range(STEP)] for t in range(STEP)]
        for t in range(STEP):
            inverse = 1.0 / small[t][t]
            for u in range(t + 1, STEP):
                ratio = small[t][u] * inverse
                lines[u] = lines[u] - ratio * lines[t]
                cols[u] = cols[u] - ratio * cols[t]
                for v in range(u, STEP):
                    small[u][v] = small[u][v] - ratio * small[t][v]
            m = m - jnp.where(at_row > j + t, cols[t] * inverse, 0.0) * lines[t]
    pivot = jnp.sum(jnp.where(at_lane == at_row, m, 0.0), axis=1, keepdims=True)
    m = m * lax.rsqrt(pivot)
    upper = jnp.where(at_lane >= at_row, m, 0.0)
    return upper[:, :HALF], m[:, HALF:]


def factor_128(a):
    u1, w1 = eliminate(a[:HALF, :HALF])
    u12 = nn(w1, a[:HALF, HALF:])
    u2, w2 = eliminate(a[HALF:, HALF:] - tn(u12, u12))
    w21 = -nn(w2, tn(u12, w1))
    zero = jnp.zeros((HALF, HALF), jnp.float32)
    u = jnp.concatenate([jnp.concatenate([u1, u12], 1), jnp.concatenate([zero, u2], 1)], 0)
    w = jnp.concatenate([jnp.concatenate([w1, zero], 1), jnp.concatenate([w21, w2], 1)], 0)
    return u, w


def solve_kernel(unfold, gram, lower, basis, upper, inverse, x_hi, x_lo, out, out_sem):
    order = upper.shape[0]
    x_hi[...], x_lo[...] = split(unfold[...])
    copies = []
    upper[...] = jnp.zeros_like(upper)
    inverse[...] = jnp.zeros_like(inverse)
    at = 0
    for left in range(0, order, LANES):
        tall = gram[at:at + order - left, :]
        upper[left:left + LANES, left:] = tall.T
        at += order - left
    for i in range(0, order, LANES):
        n = i + LANES
        u, w = factor_128(upper[i:n, i:n])
        upper[i:n, i:n] = u
        if i:
            inverse[i:n, :i] = nn(w, inverse[i:n, :i])
        inverse[i:n, i:n] = w
        w_hi, w_lo = split(inverse[i:n, :n])
        contract = ((1,), (1,))
        part = mul16(x_hi[:, :n], w_lo, contract) + mul16(x_lo[:, :n], w_hi, contract)
        b = i // LANES
        out[b] = part + mul16(x_hi[:, :n], w_hi, contract)
        copies.append(pltpu.make_async_copy(out.at[b], basis.at[:, i:n], out_sem.at[b]))
        copies[-1].start()
        if n < order:
            right = nn(w, upper[i:n, n:])
            upper[i:n, n:] = right
            for t in range(n, order, LANES):
                block = right[:, t - n:t - n + LANES]
                upper[t:t + LANES, t:] -= tn(block, right[:, t - n:])
                inverse[t:t + LANES, :n] -= tn(block, inverse[i:n, :n])
    g = lax.axis_index("ga")
    mine = lower.shape[0]
    lower[...] = upper[:, pl.ds(pl.multiple_of(g * mine, mine), mine)].T
    for copy in copies:
        copy.wait()


def shards(G, C, slab, factor):
    S, A, j_here, k_here = slab.shape
    R = factor.shape[1]
    depth, order = j_here * C, k_here * G
    s_here, a_here, chips = S // G, A // C, C // 2
    blocks = order // LANES
    cut = 8 * 2 * chips * G
    packed = -(-(blocks * (blocks + 1) // 2 * LANES) // cut) * cut
    half, quarter = packed // 2, packed // 2 // chips
    parts = 2 if a_here % 2 == 0 else 1
    sends = s_here * parts * G * C
    f32 = jnp.float32
    dma = pltpu.SemaphoreType.DMA
    unfold, gram = pl.pallas_call(
        functools.partial(exchange_kernel, G, C, parts, S * A * R),
        out_shape=(
            jax.ShapeDtypeStruct((s_here, a_here, R, order), f32),
            jax.ShapeDtypeStruct((packed, LANES), f32),
        ),
        in_specs=[pl.BlockSpec(memory_space=pl.ANY), pl.BlockSpec(memory_space=pltpu.VMEM)],
        out_specs=(pl.BlockSpec(memory_space=pltpu.VMEM), pl.BlockSpec(memory_space=pltpu.VMEM)),
        scratch_shapes=[
            pltpu.VMEM((s_here, a_here, depth, order), f32),
            pltpu.VMEM((depth, R), f32),
            pltpu.VMEM((packed, LANES), f32),
            pltpu.VMEM((half, LANES), f32),
            pltpu.VMEM((half, LANES), f32),
            pltpu.VMEM((chips, quarter, LANES), f32),
            pltpu.VMEM((quarter, LANES), f32),
            pltpu.VMEM((G, quarter // G, LANES), f32),
            dma((sends,)), dma((sends,)), dma((C,)), dma((C,)), dma((s_here * parts,)),
            dma((chips,)), dma((chips,)), dma((chips,)), dma((chips,)), dma((G,)), dma((G,)),
            dma((G,)), dma((G,)), *(dma((G * chips,)) for _ in range(4)),
        ],
        compiler_params=pltpu.CompilerParams(
            collective_id=0, has_side_effects=True, vmem_limit_bytes=40 * 1024 * 1024
        ),
    )(slab, factor)
    rows = s_here * a_here * R
    lower, basis = pl.pallas_call(
        solve_kernel,
        out_shape=(
            jax.ShapeDtypeStruct((order // G, order), f32),
            jax.ShapeDtypeStruct((rows, order), f32),
        ),
        in_specs=[pl.BlockSpec(memory_space=pltpu.VMEM)] * 2,
        out_specs=(pl.BlockSpec(memory_space=pltpu.VMEM), pl.BlockSpec(memory_space=pl.ANY)),
        scratch_shapes=[
            pltpu.VMEM((order, order), f32),
            pltpu.VMEM((order, order), f32),
            pltpu.VMEM((rows, order), jnp.bfloat16),
            pltpu.VMEM((rows, order), jnp.bfloat16),
            pltpu.VMEM((blocks, rows, LANES), f32),
            dma((blocks,)),
        ],
        compiler_params=pltpu.CompilerParams(vmem_limit_bytes=40 * 1024 * 1024),
    )(unfold.reshape(rows, order), gram)
    return lower, basis.reshape(s_here, a_here, R, order)


def solution(mesh):
    placed = (P(None, None, "sa", "ga"), P("sa", None))
    return jax.shard_map(
        functools.partial(shards, mesh.shape["ga"], mesh.shape["sa"]),
        mesh=mesh,
        in_specs=placed,
        out_specs=(P("ga", None), P("ga", "sa", None, None)),
        check_vma=False,
    )
```
